32 devices in a mesh: blk: 8 (over z, x), win: 4 (over y, core).
Axes of the slice: x: 2, y: 2, z: 4, core: 2. Of those that a mesh axis runs over, the one named last changes fastest.
Arguments:
- samples: bfloat16 [1024, 32, 2048], P('blk', 'win'), may hold values from -6 to 6
- pair_offsets: int32 [24], P('blk'), may hold values from 0 to 4, as said below
- pair_count: int32 [8], P('blk'), may hold values from 1 to 3
Outputs:
- cross_spectra: bfloat16 [24, 128, 2, 128, 128], P('blk', 'win')
The draws below stay inside these ranges and needn't reach their ends.
Inputs may be any that keep to these rules, and one draw needn't show every extreme that they name: `pair_offsets`: entry w * 3 + s belongs to worker w. The live slots of a worker (s below its count) hold different offsets, with w + offset below the number of blocks; the other slots hold 0.
All inputs are finite; a program needn't handle non-finite values.
Results may differ from the reference program's by a relative error of at most 0.0068.
Values may be sent and summed in bfloat16 or wider, within the bound.
A program may use at most 64 MiB of HBM per device.

```python
import functools
import math
import jax
import jax.numpy as jnp
from jax import lax

CH = 128
NT = 2048
BINS = 128
BIN0 = 32
SMOOTH = 4
OFFSET = 4
SLOTS = 3
WINDOWS = 32
CHANNELS = 1024
PAIR_SLOTS = 24
N_BLK = 8


def pair_table(key):
    key_count = jax.random.fold_in(key, 11)
    key_order = jax.random.fold_in(key, 12)
    key_pick = jax.random.fold_in(key, 13)
    workers = jnp.arange(N_BLK, dtype=jnp.int32)
    avail = jnp.minimum(OFFSET + 1, N_BLK - workers)
    chosen = jax.random.randint(key_pick, (), 0, N_BLK - OFFSET)
    drawn = jax.random.randint(key_count, (N_BLK,), 0, SLOTS)
    counts = 1 + drawn * drawn // SLOTS
    counts = jnp.where(workers == chosen, SLOTS, counts)
    counts = jnp.minimum(counts, avail)
    reaches = jnp.arange(OFFSET + 1, dtype=jnp.int32)
    scores = jax.random.randint(key_order, (N_BLK, OFFSET + 1), 0, 4096) * (OFFSET + 1) + reaches[None, :]
    scores = jnp.where(reaches[None, :] >= avail[:, None], scores + 4096 * (OFFSET + 1), scores)
    scores = jnp.where((workers[:, None] == chosen) & (reaches[None, :] == OFFSET), -1, scores)
    ordering = jnp.argsort(scores, axis=1, stable=True)[:, :SLOTS]
    live = jnp.arange(SLOTS, dtype=jnp.int32)[None, :] < counts[:, None]
    offsets = jnp.where(live, ordering, 0).astype(jnp.int32).reshape(-1)
    return (offsets, counts.astype(jnp.int32))


def draw_pair_offsets(key, part):
    return pair_table(key)[0]


def draw_pair_count(key, part):
    return pair_table(key)[1]


def level_of(stream_key, shape, pieces, low, largest):
    gain, own = 1.0, jax.random.fold_in(stream_key, 6)
    for axis_at, shards_of in pieces:
        heights = jnp.exp(jax.random.uniform(jax.random.fold_in(own, axis_at), (shards_of,), jnp.float32, low / len(pieces), largest / len(pieces)))
        gain = gain * jnp.repeat(heights, shape[axis_at] // shards_of).reshape([-1 if axis == axis_at else 1 for axis in range(len(shape))])
    return gain


def centred(own_key, shape, deviation, most, shards=(), kind=jnp.bfloat16):
    entries = jax.random.normal(own_key, shape, jnp.float32) * deviation
    if len(shards) > 0:
        entries = level_of(own_key, shape, shards, -0.22, 0.18) * entries
    return jnp.clip(entries, min=-most, max=most).astype(kind)


def setup_inputs(seed: int = 0) -> dict:
    key_list = jax.random.split(jax.random.key(seed), 4)
    return {
        "samples": centred(key_list[0], (CHANNELS, WINDOWS, NT), 1.0, 6.0, ((0, 8), (1, 4))),
        "pair_offsets": draw_pair_offsets(jax.random.fold_in(key_list[3], 71), 0),
        "pair_count": draw_pair_count(jax.random.fold_in(key_list[3], 71), 0),
    }


water_level = 0.1
epsilon = 1e-06

def dft_table(length):
    sample_idx = jnp.arange(length, dtype=jnp.int32)
    bin_freqs = BIN0 + jnp.arange(BINS, dtype=jnp.int32)
    phases = sample_idx[:, None] * bin_freqs[None, :] % length
    angles = phases.astype(jnp.float32) * (2.0 * math.pi / length)
    window_taper = 0.5 - 0.5 * jnp.cos((sample_idx.astype(jnp.float32) + 0.5) * (2.0 * math.pi / length))
    cosines = window_taper[:, None] * jnp.cos(angles)
    sines = -window_taper[:, None] * jnp.sin(angles)
    return jnp.concatenate([cosines, sines], axis=1).astype(jnp.bfloat16)

def band_weights():
    bin_index = jnp.arange(BINS, dtype=jnp.int32)
    inside = (jnp.abs(bin_index[:, None] - bin_index[None, :]) <= SMOOTH).astype(jnp.float32)
    return inside / lax.optimization_barrier(jnp.sum(inside, axis=0, keepdims=True))

def whiten_block(block, table, weights):
    channels, win_count, length = block.shape
    spectrum = jnp.einsum('cwt,tk->wkc', block.astype(jnp.float32), table.astype(jnp.float32), precision=lax.Precision.HIGHEST)
    spectrum = spectrum.reshape(win_count, 2, BINS, channels)
    energy = spectrum[:, 0] * spectrum[:, 0] + spectrum[:, 1] * spectrum[:, 1]
    smoothed = jnp.einsum('wjc,jb->wbc', energy, weights, precision=lax.Precision.HIGHEST)
    average = lax.optimization_barrier(jnp.mean(energy, axis=1, keepdims=True))
    factor = lax.rsqrt(smoothed + water_level * average + epsilon)
    return (spectrum * factor[:, None]).astype(jnp.bfloat16)

def reference(samples, pair_offsets, pair_count):
    table = dft_table(NT)
    weights = band_weights()
    blocks = samples.reshape(N_BLK, CH, WINDOWS, NT)
    whitened = lax.map(functools.partial(whiten_block, table=table, weights=weights), blocks)

    def one_slot(position):
        worker = position // SLOTS
        slot_rank = position % SLOTS
        distance = pair_offsets[position]
        live = slot_rank < pair_count[worker]
        first = lax.dynamic_index_in_dim(whitened, worker, 0, keepdims=False).astype(jnp.float32)
        partner = jnp.minimum(worker + distance, N_BLK - 1).astype(jnp.int32)
        second = lax.dynamic_index_in_dim(whitened, partner, 0, keepdims=False).astype(jnp.float32)
        highest = lax.Precision.HIGHEST
        real_part = jnp.einsum('wbi,wbj->bij', first[:, 0], second[:, 0], precision=highest) + jnp.einsum('wbi,wbj->bij', first[:, 1], second[:, 1], precision=highest)
        imag_part = jnp.einsum('wbi,wbj->bij', first[:, 1], second[:, 0], precision=highest) - jnp.einsum('wbi,wbj->bij', first[:, 0], second[:, 1], precision=highest)
        stacked = jnp.stack([real_part, imag_part], axis=1) * (1.0 / WINDOWS)
        return jnp.where(live, stacked, jnp.zeros_like(stacked)).astype(jnp.bfloat16)
    return lax.map(one_slot, jnp.arange(PAIR_SLOTS, dtype=jnp.int32))
```

```python
import functools
import math

import jax
import jax.numpy as jnp
import ml_dtypes
import numpy as np
from jax import lax
from jax.experimental import pallas as pl
from jax.experimental.pallas import tpu as pltpu
from jax.sharding import PartitionSpec as P

BINS = 128
BIN0 = 32
SMOOTH = 4
OFFSET = 4

WATER_LEVEL = 0.1
EPSILON = 1e-06

ROW_STEPS = 4
CHUNKS = 4
BIN_BLOCK = 4
VMEM_LIMIT = 40 * 1024 * 1024
MESH = pl.DeviceIdType.MESH


def dft_table(length):
    sample_idx = np.arange(length, dtype=np.int64)
    bin_freqs = BIN0 + np.arange(BINS, dtype=np.int64)
    angles = (sample_idx[:, None] * bin_freqs[None, :] % length) * (2.0 * math.pi / length)
    taper = 0.5 - 0.5 * np.cos((sample_idx + 0.5) * (2.0 * math.pi / length))
    table = np.concatenate(
        [taper[:, None] * np.cos(angles), -taper[:, None] * np.sin(angles)], axis=1
    )
    return table.astype(np.float32).astype(ml_dtypes.bfloat16)


def band_table():
    idx = np.arange(BINS)
    inside = (np.abs(idx[:, None] - idx[None, :]) <= SMOOTH).astype(np.float32)
    band = np.concatenate([inside, np.ones((BINS, BINS), np.float32)], axis=1)
    scale = np.concatenate(
        [1.0 / inside.sum(axis=0), np.full((BINS,), WATER_LEVEL / BINS, np.float32)]
    )
    return band.astype(ml_dtypes.bfloat16), scale.astype(np.float32)[None, :]


def whiten_kernel(wins, samples_ref, table_ref, band_ref, scale_ref, out_ref, white, turned):
    step = pl.program_id(0)
    rows = samples_ref.shape[0]
    channels = white.shape[1] // wins
    spectrum = jnp.dot(samples_ref[...], table_ref[...], preferred_element_type=jnp.float32)
    real, imag = spectrum[:, :BINS], spectrum[:, BINS:]
    energy = real * real + imag * imag
    sums = jnp.dot(
        energy.astype(jnp.bfloat16), band_ref[...], preferred_element_type=jnp.float32
    ) * scale_ref[...]
    factor = lax.rsqrt(sums[:, :BINS] + sums[:, BINS:] + EPSILON)
    here = pl.ds(pl.multiple_of(step * rows, rows), rows)
    white[0, here, :] = real * factor
    white[1, here, :] = imag * factor

    @pl.when(step == pl.num_programs(0) - 1)
    def _():
        for part in range(2):
            for win in range(wins):
                piece = white[part, pl.ds(win, channels, stride=wins), :]
                turned[pl.ds(part * wins + win, BINS, stride=2 * wins), :] = piece.T
        out_ref[...] = turned[...].reshape(out_ref.shape).astype(jnp.bfloat16)


def whiten(samples):
    channels, wins, length = samples.shape
    rows = channels * wins
    table = jnp.asarray(dft_table(length))
    band, scale = band_table()
    step_rows = rows // ROW_STEPS
    return pl.pallas_call(
        functools.partial(whiten_kernel, wins),
        grid=(ROW_STEPS,),
        in_specs=[
            pl.BlockSpec((step_rows, length), lambda i: (i, 0)),
            pl.BlockSpec((length, 2 * BINS), lambda i: (0, 0)),
            pl.BlockSpec((BINS, 2 * BINS), lambda i: (0, 0)),
            pl.BlockSpec((1, 2 * BINS), lambda i: (0, 0)),
        ],
        out_specs=pl.BlockSpec((BINS, 2 * wins, channels), lambda i: (0, 0, 0)),
        out_shape=jax.ShapeDtypeStruct((BINS, 2 * wins, channels), jnp.bfloat16),
        scratch_shapes=[
            pltpu.VMEM((2, rows, BINS), jnp.float32),
            pltpu.VMEM((BINS * 2 * wins, channels), jnp.float32),
        ],
        compiler_params=pltpu.CompilerParams(vmem_limit_bytes=VMEM_LIMIT),
        name="whiten",
    )(samples.reshape(rows, length), table, jnp.asarray(band), jnp.asarray(scale))


def exchange_kernel(
    nb, nw, send_ref, near_ref, home_sem, a_send, a_recv, z_send, z_recv, x_send, x_recv
):
    worker, group = lax.axis_index("blk"), lax.axis_index("win")
    level, odd = lax.div(worker, 2), lax.rem(worker, 2)
    levels = nb // 2
    partner = worker + 1 - 2 * odd
    has_below = level >= 1
    has_one = level + 1 < levels
    has_two = level + 2 < levels
    is_even, is_odd = odd == 0, odd == 1
    bins_dev = near_ref.shape[1]
    rows = send_ref.shape[1]
    size = bins_dev // CHUNKS

    barrier = pltpu.get_barrier_semaphore()

    def greet(device):
        pl.semaphore_signal(barrier, inc=1, device_id=device, device_id_type=MESH)

    peers = [lax.rem(group + k, nw) for k in range(1, nw)]
    for peer in peers:
        greet({"win": peer})
    greet({"blk": partner})

    @pl.when(has_below)
    def _():
        greet({"blk": worker - 2})

    @pl.when(has_one)
    def _():
        greet({"blk": worker + 2})

    my_rows = pl.ds(pl.multiple_of(group * rows, rows), rows)
    home = pltpu.make_async_copy(
        send_ref.at[pl.ds(group * bins_dev, bins_dev)], near_ref.at[0, :, my_rows], home_sem
    )
    home.start()
    pl.semaphore_wait(barrier, nw + has_below.astype(jnp.int32) + has_one.astype(jnp.int32))

    def spread(k, c):
        return pltpu.make_async_remote_copy(
            src_ref=send_ref.at[pl.ds(peers[k] * bins_dev + c * size, size)],
            dst_ref=near_ref.at[0, pl.ds(c * size, size), my_rows],
            send_sem=a_send.at[k, c],
            recv_sem=a_recv.at[k, c],
            device_id={"win": peers[k]},
            device_id_type=MESH,
        )

    def move(src, dst, device, send, recv, at, c):
        return pltpu.make_async_remote_copy(
            src_ref=near_ref.at[src, pl.ds(c * size, size)],
            dst_ref=near_ref.at[dst, pl.ds(c * size, size)],
            send_sem=send.at[at, c],
            recv_sem=recv.at[at, c],
            device_id={"blk": device},
            device_id_type=MESH,
        )

    def down(at, c):
        return move(2 * at, 2 * at + 2, worker - 2, z_send, z_recv, at, c)

    def across(at, c):
        return move(2 * at + 2 * (1 - odd), 2 * at + 1, partner, x_send, x_recv, at, c)

    for c in range(CHUNKS):
        for k in range(nw - 1):
            spread(k, c).start()
    home.wait()

    def own_part(c):
        for k in range(nw - 1):
            spread(k, c).wait_recv()

        @pl.when(has_below)
        def _():
            down(0, c).start()

        @pl.when(is_odd)
        def _():
            across(0, c).start()

    def second_part(c):
        @pl.when(has_one)
        def _():
            down(0, c).wait_recv()

            @pl.when(has_below)
            def _():
                down(1, c).start()

            @pl.when(is_even)
            def _():
                across(0, c).start()

            @pl.when(is_odd)
            def _():
                across(1, c).start()

    def fourth_part(c):
        @pl.when(has_two)
        def _():
            down(1, c).wait_recv()

            @pl.when(is_even)
            def _():
                across(1, c).start()

    own_part(0)
    for c in range(1, CHUNKS):
        own_part(c)
        second_part(c - 1)
    second_part(CHUNKS - 1)
    for c in range(CHUNKS):
        fourth_part(c)

    first_live = jnp.logical_or(is_even, has_one)
    third_live = jnp.logical_or(jnp.logical_and(is_even, has_one), has_two)
    first_sent = jnp.logical_or(is_odd, has_one)
    third_sent = jnp.logical_or(jnp.logical_and(is_odd, has_one), has_two)
    both = jnp.logical_and(has_below, has_one)
    for c in range(CHUNKS):
        for k in range(nw - 1):
            spread(k, c).wait_send()

        @pl.when(first_live)
        def _():
            across(0, c).wait_recv()

        @pl.when(third_live)
        def _():
            across(1, c).wait_recv()

        @pl.when(has_below)
        def _():
            down(0, c).wait_send()

        @pl.when(both)
        def _():
            down(1, c).wait_send()

        @pl.when(first_sent)
        def _():
            across(0, c).wait_send()

        @pl.when(third_sent)
        def _():
            across(1, c).wait_send()


def exchange(white, nb, nw):
    bins, rows, channels = white.shape
    return pl.pallas_call(
        functools.partial(exchange_kernel, nb, nw),
        in_specs=[pl.BlockSpec(memory_space=pl.ANY)],
        out_specs=pl.BlockSpec(memory_space=pl.ANY),
        out_shape=jax.ShapeDtypeStruct(
            (OFFSET + 1, bins // nw, nw * rows, channels), jnp.bfloat16
        ),
        scratch_shapes=[
            pltpu.SemaphoreType.DMA,
            pltpu.SemaphoreType.DMA((nw - 1, CHUNKS)),
            pltpu.SemaphoreType.DMA((nw - 1, CHUNKS)),
            pltpu.SemaphoreType.DMA((2, CHUNKS)),
            pltpu.SemaphoreType.DMA((2, CHUNKS)),
            pltpu.SemaphoreType.DMA((2, CHUNKS)),
            pltpu.SemaphoreType.DMA((2, CHUNKS)),
        ],
        compiler_params=pltpu.CompilerParams(collective_id=0, has_side_effects=True),
        name="exchange",
    )(white)


def cross_kernel(half, windows, offsets_ref, count_ref, own_ref, *refs):
    partners, out_ref = refs[:-1], refs[-1]
    scales = [
        jnp.where(s < count_ref[0], 1.0 / windows, 0.0).astype(jnp.float32)
        for s in range(len(partners))
    ]
    depth, channels = own_ref.shape[2], own_ref.shape[3]
    for b in range(own_ref.shape[1]):
        mine = own_ref[0, b].astype(jnp.float32)
        split = mine.reshape(depth // (2 * half), 2, half, channels)
        swapped = jnp.stack([split[:, 1], -split[:, 0]], axis=1).reshape(depth, channels)
        left = jnp.concatenate([mine.T, swapped.T], axis=0).astype(jnp.bfloat16)
        for s, partner in enumerate(partners):
            value = jnp.dot(left, partner[0, b], preferred_element_type=jnp.float32) * scales[s]
            out_ref[s, b] = value.reshape(2, channels, channels).astype(jnp.bfloat16)


def cross(near, pair_offsets, pair_count, wins):
    _, bins_dev, depth, channels = near.shape
    slots = pair_offsets.shape[0]

    def partner_spec(s):
        return pl.BlockSpec(
            (1, BIN_BLOCK, depth, channels), lambda i, offsets, count: (offsets[s], i, 0, 0)
        )

    return pl.pallas_call(
        functools.partial(cross_kernel, wins, depth // 2),
        grid_spec=pltpu.PrefetchScalarGridSpec(
            num_scalar_prefetch=2,
            grid=(bins_dev // BIN_BLOCK,),
            in_specs=[
                pl.BlockSpec((1, BIN_BLOCK, depth, channels), lambda i, offsets, count: (0, i, 0, 0))
            ]
            + [partner_spec(s) for s in range(slots)],
            out_specs=pl.BlockSpec(
                (slots, BIN_BLOCK, 2, channels, channels),
                lambda i, offsets, count: (0, i, 0, 0, 0),
            ),
        ),
        out_shape=jax.ShapeDtypeStruct((slots, bins_dev, 2, channels, channels), jnp.bfloat16),
        compiler_params=pltpu.CompilerParams(vmem_limit_bytes=VMEM_LIMIT),
        name="cross",
    )(pair_offsets, pair_count, *([near] * (slots + 1)))


def shards(nb, nw, samples, pair_offsets, pair_count):
    white = whiten(samples)
    near = exchange(white, nb, nw)
    return cross(near, pair_offsets, pair_count, samples.shape[1])


def solution(mesh):
    body = functools.partial(shards, mesh.shape["blk"], mesh.shape["win"])
    in_specs = (P("blk", "win", None), P("blk"), P("blk"))
    out_specs = P("blk", "win", None, None, None)
    return jax.shard_map(body, mesh=mesh, in_specs=in_specs, out_specs=out_specs, check_vma=False)
```

```python
import functools
import math

import jax
import jax.numpy as jnp
import ml_dtypes
import numpy as np
from jax import lax
from jax.experimental import pallas as pl
from jax.experimental.pallas import tpu as pltpu
from jax.sharding import PartitionSpec as P

BINS = 128
BIN0 = 32
SMOOTH = 4
OFFSET = 4

WATER_LEVEL = 0.1
EPSILON = 1e-06

ROW_STEPS = 4
CHUNKS = 8
AHEAD = 2
LAG = 2
DEPTH = 2
BIN_BLOCK = 4
VMEM_LIMIT = 60 * 1024 * 1024
CROSS_LIMIT = 40 * 1024 * 1024
SMALL_LIMIT = 4 * 1024 * 1024
MESH = pl.DeviceIdType.MESH


def dft_table(length):
    sample_idx = np.arange(length, dtype=np.int64)
    bin_freqs = BIN0 + np.arange(BINS, dtype=np.int64)
    angles = (sample_idx[:, None] * bin_freqs[None, :] % length) * (2.0 * math.pi / length)
    taper = 0.5 - 0.5 * np.cos((sample_idx + 0.5) * (2.0 * math.pi / length))
    table = np.concatenate(
        [taper[:, None] * np.cos(angles), -taper[:, None] * np.sin(angles)], axis=1
    )
    return table.astype(np.float32).astype(ml_dtypes.bfloat16)


def band_weights():
    source = lax.broadcasted_iota(jnp.int32, (BINS, 2 * BINS), 0)
    target = lax.broadcasted_iota(jnp.int32, (BINS, 2 * BINS), 1)
    inside = jnp.logical_or(jnp.abs(source - target) <= SMOOTH, target >= BINS)
    return jnp.where(inside, 1.0, 0.0).astype(jnp.bfloat16)


def band_scale():
    bin_index = lax.broadcasted_iota(jnp.int32, (1, 2 * BINS), 1)
    inside = jnp.minimum(bin_index, SMOOTH) + jnp.minimum(BINS - 1 - bin_index, SMOOTH) + 1
    share = 1.0 / jnp.maximum(inside, 1).astype(jnp.float32)
    return jnp.where(bin_index < BINS, share, WATER_LEVEL / BINS)


def whiten_kernel(wins, samples_ref, table_ref, out_ref, white, turned):
    step = pl.program_id(0)
    rows = samples_ref.shape[0]
    channels = white.shape[1] // wins
    spectrum = jnp.dot(samples_ref[...], table_ref[...], preferred_element_type=jnp.float32)
    real, imag = spectrum[:, :BINS], spectrum[:, BINS:]
    energy = real * real + imag * imag
    high = energy.astype(jnp.bfloat16)
    low = (energy - high.astype(jnp.float32)).astype(jnp.bfloat16)
    weights = band_weights()
    sums = jnp.dot(high, weights, preferred_element_type=jnp.float32)
    sums += jnp.dot(low, weights, preferred_element_type=jnp.float32)
    sums *= band_scale()
    factor = lax.rsqrt(sums[:, :BINS] + sums[:, BINS:] + EPSILON)
    here = pl.ds(pl.multiple_of(step * rows, rows), rows)
    white[0, here, :] = real * factor
    white[1, here, :] = imag * factor

    @pl.when(step == pl.num_programs(0) - 1)
    def _():
        for part in range(2):
            for win in range(wins):
                piece = white[part, pl.ds(win, channels, stride=wins), :]
                turned[pl.ds(part * wins + win, BINS, stride=2 * wins), :] = piece.T
        out_ref[...] = turned[...].reshape(out_ref.shape).astype(jnp.bfloat16)


def whiten(samples):
    channels, wins, length = samples.shape
    rows = channels * wins
    table = jnp.asarray(dft_table(length))
    step_rows = rows // ROW_STEPS
    return pl.pallas_call(
        functools.partial(whiten_kernel, wins),
        grid=(ROW_STEPS,),
        in_specs=[
            pl.BlockSpec((step_rows, length), lambda i: (i, 0)),
            pl.BlockSpec((length, 2 * BINS), lambda i: (0, 0)),
        ],
        out_specs=pl.BlockSpec((BINS, 2 * wins, channels), lambda i: (0, 0, 0)),
        out_shape=jax.ShapeDtypeStruct((BINS, 2 * wins, channels), jnp.bfloat16),
        scratch_shapes=[
            pltpu.VMEM((2, rows, BINS), jnp.float32),
            pltpu.VMEM((BINS * 2 * wins, channels), jnp.float32),
        ],
        compiler_params=pltpu.CompilerParams(vmem_limit_bytes=VMEM_LIMIT),
        name="whiten",
    )(samples.reshape(rows, length), table)


def exchange_kernel(
    nb, nw, send_ref, near_ref, home_sem, a_send, a_recv, z_send, z_recv, x_send, x_recv
):
    worker, group = lax.axis_index("blk"), lax.axis_index("win")
    level, odd = lax.div(worker, 2), lax.rem(worker, 2)
    levels = nb // 2
    partner = worker + 1 - 2 * odd
    has_below = level >= 1
    has_one = level + 1 < levels
    has_two = level + 2 < levels
    is_even, is_odd = odd == 0, odd == 1
    bins_dev = near_ref.shape[1]
    rows = send_ref.shape[1]
    size = bins_dev // CHUNKS

    barrier = pltpu.get_barrier_semaphore()

    def greet(device):
        pl.semaphore_signal(barrier, inc=1, device_id=device, device_id_type=MESH)

    peers = [lax.rem(group + k, nw) for k in range(1, nw)]
    for peer in peers:
        greet({"win": peer})
    greet({"blk": partner})

    @pl.when(has_below)
    def _():
        greet({"blk": worker - 2})

    @pl.when(has_one)
    def _():
        greet({"blk": worker + 2})

    my_rows = pl.ds(pl.multiple_of(group * rows, rows), rows)
    home = pltpu.make_async_copy(
        send_ref.at[pl.ds(group * bins_dev, bins_dev)], near_ref.at[0, :, my_rows], home_sem
    )
    home.start()
    pl.semaphore_wait(barrier, nw + has_below.astype(jnp.int32) + has_one.astype(jnp.int32))

    def spread(k, c):
        return pltpu.make_async_remote_copy(
            src_ref=send_ref.at[pl.ds(peers[k] * bins_dev + c * size, size)],
            dst_ref=near_ref.at[0, pl.ds(c * size, size), my_rows],
            send_sem=a_send.at[k, c],
            recv_sem=a_recv.at[k, c],
            device_id={"win": peers[k]},
            device_id_type=MESH,
        )

    def move(src, dst, device, send, recv, at, c):
        return pltpu.make_async_remote_copy(
            src_ref=near_ref.at[src, pl.ds(c * size, size)],
            dst_ref=near_ref.at[dst, pl.ds(c * size, size)],
            send_sem=send.at[at, c],
            recv_sem=recv.at[at, c],
            device_id={"blk": device},
            device_id_type=MESH,
        )

    def down(at, c):
        return move(2 * at, 2 * at + 2, worker - 2, z_send, z_recv, at, c)

    def across(at, c):
        return move(2 * at + 2 * (1 - odd), 2 * at + 1, partner, x_send, x_recv, at, c)

    both = jnp.logical_and(has_below, has_one)
    odd_one = jnp.logical_and(is_odd, has_one)
    even_one = jnp.logical_and(is_even, has_one)
    even_two = jnp.logical_and(is_even, has_two)
    items = 2 * CHUNKS

    def sends(t):
        found = []
        if 0 <= t < items:
            at, c = divmod(t, CHUNKS)
            found.append(((has_below, both)[at], down(at, c)))
            found.append(((is_odd, odd_one)[at], across(at, c)))
        if 0 <= t - LAG < items:
            at, c = divmod(t - LAG, CHUNKS)
            found.append(((even_one, even_two)[at], across(at, c)))
        return found

    def guarded(when, action):
        @pl.when(when)
        def _():
            action()

    def start_spread(c):
        if c < CHUNKS:
            for k in range(nw - 1):
                spread(k, c).start()

    for c in range(AHEAD):
        start_spread(c)
    home.wait()
    steps = items + LAG
    for t in range(steps):
        if t < CHUNKS:
            start_spread(t + AHEAD)
            for k in range(nw - 1):
                spread(k, t).wait_recv()
        if 0 <= t - LAG < items:
            at, c = divmod(t - LAG, CHUNKS)
            guarded((has_one, has_two)[at], down(at, c).wait_recv)
        for when, copy in sends(t - DEPTH):
            guarded(when, copy.wait_send)
        for when, copy in sends(t):
            guarded(when, copy.start)
    for t in range(steps - DEPTH, steps):
        for when, copy in sends(t):
            guarded(when, copy.wait_send)
    first_live = jnp.logical_or(is_even, has_one)
    third_live = jnp.logical_or(even_one, has_two)
    for c in range(CHUNKS):
        for k in range(nw - 1):
            spread(k, c).wait_send()
        guarded(first_live, across(0, c).wait_recv)
        guarded(third_live, across(1, c).wait_recv)


def exchange(white, nb, nw):
    bins, rows, channels = white.shape
    return pl.pallas_call(
        functools.partial(exchange_kernel, nb, nw),
        in_specs=[pl.BlockSpec(memory_space=pl.ANY)],
        out_specs=pl.BlockSpec(memory_space=pl.ANY),
        out_shape=jax.ShapeDtypeStruct(
            (OFFSET + 1, bins // nw, nw * rows, channels), jnp.bfloat16
        ),
        scratch_shapes=[
            pltpu.SemaphoreType.DMA,
            pltpu.SemaphoreType.DMA((nw - 1, CHUNKS)),
            pltpu.SemaphoreType.DMA((nw - 1, CHUNKS)),
            pltpu.SemaphoreType.DMA((2, CHUNKS)),
            pltpu.SemaphoreType.DMA((2, CHUNKS)),
            pltpu.SemaphoreType.DMA((2, CHUNKS)),
            pltpu.SemaphoreType.DMA((2, CHUNKS)),
        ],
        compiler_params=pltpu.CompilerParams(
            collective_id=0, has_side_effects=True, vmem_limit_bytes=SMALL_LIMIT
        ),
        name="exchange",
    )(white)


def cross_kernel(half, windows, offsets_ref, count_ref, own_ref, *refs):
    partners, out_ref = refs[:-1], refs[-1]
    scales = [
        jnp.where(s < count_ref[0], 1.0 / windows, 0.0).astype(jnp.float32)
        for s in range(len(partners))
    ]
    depth, channels = own_ref.shape[2], own_ref.shape[3]
    for b in range(own_ref.shape[1]):
        left = own_ref[0, b].astype(jnp.float32).T.astype(jnp.bfloat16)
        for s, partner in enumerate(partners):
            right = partner[0, b].astype(jnp.float32) * scales[s]
            split = right.reshape(depth // (2 * half), 2, half, channels)
            turned = jnp.stack([-split[:, 1], split[:, 0]], axis=1).reshape(depth, channels)
            right = jnp.concatenate([right, turned], axis=1).astype(jnp.bfloat16)
            value = jnp.dot(left, right, preferred_element_type=jnp.float32)
            value = value.astype(jnp.bfloat16)
            out_ref[s, b, 0] = value[:, :channels]
            out_ref[s, b, 1] = value[:, channels:]


def cross(near, pair_offsets, pair_count, wins):
    _, bins_dev, depth, channels = near.shape
    slots = pair_offsets.shape[0]

    def partner_spec(s):
        return pl.BlockSpec(
            (1, BIN_BLOCK, depth, channels), lambda i, offsets, count: (offsets[s], i, 0, 0)
        )

    return pl.pallas_call(
        functools.partial(cross_kernel, wins, depth // 2),
        grid_spec=pltpu.PrefetchScalarGridSpec(
            num_scalar_prefetch=2,
            grid=(bins_dev // BIN_BLOCK,),
            in_specs=[
                pl.BlockSpec((1, BIN_BLOCK, depth, channels), lambda i, offsets, count: (0, i, 0, 0))
            ]
            + [partner_spec(s) for s in range(slots)],
            out_specs=pl.BlockSpec(
                (slots, BIN_BLOCK, 2, channels, channels),
                lambda i, offsets, count: (0, i, 0, 0, 0),
            ),
        ),
        out_shape=jax.ShapeDtypeStruct((slots, bins_dev, 2, channels, channels), jnp.bfloat16),
        compiler_params=pltpu.CompilerParams(vmem_limit_bytes=CROSS_LIMIT),
        name="cross",
    )(pair_offsets, pair_count, *([near] * (slots + 1)))


def shards(nb, nw, samples, pair_offsets, pair_count):
    white = whiten(samples)
    near = exchange(white, nb, nw)
    return cross(near, pair_offsets, pair_count, samples.shape[1])


def solution(mesh):
    body = functools.partial(shards, mesh.shape["blk"], mesh.shape["win"])
    in_specs = (P("blk", "win", None), P("blk"), P("blk"))
    out_specs = P("blk", "win", None, None, None)
    return jax.shard_map(body, mesh=mesh, in_specs=in_specs, out_specs=out_specs, check_vma=False)
```

```python
import functools
import math

import jax
import jax.numpy as jnp
import ml_dtypes
import numpy as np
from jax import lax
from jax.experimental import pallas as pl
from jax.experimental.pallas import tpu as pltpu
from jax.sharding import PartitionSpec as P

BINS = 128
BIN0 = 32
SMOOTH = 4
OFFSET = 4

WATER_LEVEL = 0.1
EPSILON = 1e-06

ROW_STEPS = 2
CHUNKS = 8
AHEAD = 2
LAG = 2
DEPTH = 2
BIN_BLOCK = 16
VMEM_LIMIT = 60 * 1024 * 1024
CROSS_LIMIT = 40 * 1024 * 1024
SMALL_LIMIT = 4 * 1024 * 1024
MESH = pl.DeviceIdType.MESH


def dft_table(length):
    sample_idx = np.arange(length, dtype=np.int64)
    bin_freqs = BIN0 + np.arange(BINS, dtype=np.int64)
    angles = (sample_idx[:, None] * bin_freqs[None, :] % length) * (2.0 * math.pi / length)
    taper = 0.5 - 0.5 * np.cos((sample_idx + 0.5) * (2.0 * math.pi / length))
    table = np.concatenate(
        [taper[:, None] * np.cos(angles), -taper[:, None] * np.sin(angles)], axis=1
    )
    return table.astype(np.float32).astype(ml_dtypes.bfloat16)


def band_weights():
    source = lax.broadcasted_iota(jnp.int32, (BINS, 2 * BINS), 0)
    target = lax.broadcasted_iota(jnp.int32, (BINS, 2 * BINS), 1)
    inside = jnp.logical_or(jnp.abs(source - target) <= SMOOTH, target >= BINS)
    return jnp.where(inside, 1.0, 0.0).astype(jnp.bfloat16)


def band_scale():
    bin_index = lax.broadcasted_iota(jnp.int32, (1, 2 * BINS), 1)
    inside = jnp.minimum(bin_index, SMOOTH) + jnp.minimum(BINS - 1 - bin_index, SMOOTH) + 1
    share = 1.0 / jnp.maximum(inside, 1).astype(jnp.float32)
    return jnp.where(bin_index < BINS, share, WATER_LEVEL / BINS)


def whiten_kernel(wins, samples_ref, table_ref, out_ref, white, turned):
    step = pl.program_id(0)
    rows = samples_ref.shape[0]
    channels = white.shape[1] // wins
    spectrum = jnp.dot(samples_ref[...], table_ref[...], preferred_element_type=jnp.float32)
    real, imag = spectrum[:, :BINS], spectrum[:, BINS:]
    energy = real * real + imag * imag
    high = energy.astype(jnp.bfloat16)
    low = (energy - high.astype(jnp.float32)).astype(jnp.bfloat16)
    weights = band_weights()
    sums = jnp.dot(high, weights, preferred_element_type=jnp.float32)
    sums += jnp.dot(low, weights, preferred_element_type=jnp.float32)
    sums *= band_scale()
    factor = lax.rsqrt(sums[:, :BINS] + sums[:, BINS:] + EPSILON)
    here = pl.ds(pl.multiple_of(step * rows, rows), rows)
    white[0, here, :] = real * factor
    white[1, here, :] = imag * factor

    @pl.when(step == pl.num_programs(0) - 1)
    def _():
        for part in range(2):
            for win in range(wins):
                piece = white[part, pl.ds(win, channels, stride=wins), :]
                turned[pl.ds(part * wins + win, BINS, stride=2 * wins), :] = piece.T
        out_ref[...] = turned[...].reshape(out_ref.shape).astype(jnp.bfloat16)


def whiten(samples):
    channels, wins, length = samples.shape
    rows = channels * wins
    table = jnp.asarray(dft_table(length))
    step_rows = rows // ROW_STEPS
    return pl.pallas_call(
        functools.partial(whiten_kernel, wins),
        grid=(ROW_STEPS,),
        in_specs=[
            pl.BlockSpec((step_rows, length), lambda i: (i, 0)),
            pl.BlockSpec((length, 2 * BINS), lambda i: (0, 0)),
        ],
        out_specs=pl.BlockSpec((BINS, 2 * wins, channels), lambda i: (0, 0, 0)),
        out_shape=jax.ShapeDtypeStruct((BINS, 2 * wins, channels), jnp.bfloat16),
        scratch_shapes=[
            pltpu.VMEM((2, rows, BINS), jnp.float32),
            pltpu.VMEM((BINS * 2 * wins, channels), jnp.float32),
        ],
        compiler_params=pltpu.CompilerParams(vmem_limit_bytes=VMEM_LIMIT),
        name="whiten",
    )(samples.reshape(rows, length), table)


def exchange_kernel(
    nb, nw, send_ref, near_ref, home_sem, a_send, a_recv, z_send, z_recv, x_send, x_recv
):
    worker, group = lax.axis_index("blk"), lax.axis_index("win")
    level, odd = lax.div(worker, 2), lax.rem(worker, 2)
    levels = nb // 2
    partner = worker + 1 - 2 * odd
    has_below = level >= 1
    has_one = level + 1 < levels
    has_two = level + 2 < levels
    is_even, is_odd = odd == 0, odd == 1
    bins_dev = near_ref.shape[1]
    rows = send_ref.shape[1]
    size = bins_dev // CHUNKS

    barrier = pltpu.get_barrier_semaphore()

    def greet(device):
        pl.semaphore_signal(barrier, inc=1, device_id=device, device_id_type=MESH)

    peers = [lax.rem(group + k, nw) for k in range(1, nw)]
    for peer in peers:
        greet({"win": peer})
    greet({"blk": partner})

    @pl.when(has_below)
    def _():
        greet({"blk": worker - 2})

    @pl.when(has_one)
    def _():
        greet({"blk": worker + 2})

    my_rows = pl.ds(pl.multiple_of(group * rows, rows), rows)
    home = pltpu.make_async_copy(
        send_ref.at[pl.ds(group * bins_dev, bins_dev)], near_ref.at[0, :, my_rows], home_sem
    )
    home.start()
    pl.semaphore_wait(barrier, nw + has_below.astype(jnp.int32) + has_one.astype(jnp.int32))

    def spread(k, c):
        return pltpu.make_async_remote_copy(
            src_ref=send_ref.at[pl.ds(peers[k] * bins_dev + c * size, size)],
            dst_ref=near_ref.at[0, pl.ds(c * size, size), my_rows],
            send_sem=a_send.at[k, c],
            recv_sem=a_recv.at[k, c],
            device_id={"win": peers[k]},
            device_id_type=MESH,
        )

    def move(src, dst, device, send, recv, at, c):
        return pltpu.make_async_remote_copy(
            src_ref=near_ref.at[src, pl.ds(c * size, size)],
            dst_ref=near_ref.at[dst, pl.ds(c * size, size)],
            send_sem=send.at[at, c],
            recv_sem=recv.at[at, c],
            device_id={"blk": device},
            device_id_type=MESH,
        )

    def down(at, c):
        return move(2 * at, 2 * at + 2, worker - 2, z_send, z_recv, at, c)

    def across(at, c):
        return move(2 * at + 2 * (1 - odd), 2 * at + 1, partner, x_send, x_recv, at, c)

    both = jnp.logical_and(has_below, has_one)
    odd_one = jnp.logical_and(is_odd, has_one)
    even_one = jnp.logical_and(is_even, has_one)
    even_two = jnp.logical_and(is_even, has_two)
    items = 2 * CHUNKS

    def sends(t):
        found = []
        if 0 <= t < items:
            at, c = divmod(t, CHUNKS)
            found.append(((has_below, both)[at], down(at, c)))
            found.append(((is_odd, odd_one)[at], across(at, c)))
        if 0 <= t - LAG < items:
            at, c = divmod(t - LAG, CHUNKS)
            found.append(((even_one, even_two)[at], across(at, c)))
        return found

    def guarded(when, action):
        @pl.when(when)
        def _():
            action()

    def start_spread(c):
        if c < CHUNKS:
            for k in range(nw - 1):
                spread(k, c).start()

    for c in range(AHEAD):
        start_spread(c)
    home.wait()
    steps = items + LAG
    for t in range(steps):
        if t < CHUNKS:
            start_spread(t + AHEAD)
            for k in range(nw - 1):
                spread(k, t).wait_recv()
        if 0 <= t - LAG < items:
            at, c = divmod(t - LAG, CHUNKS)
            guarded((has_one, has_two)[at], down(at, c).wait_recv)
        for when, copy in sends(t - DEPTH):
            guarded(when, copy.wait_send)
        for when, copy in sends(t):
            guarded(when, copy.start)
    for t in range(steps - DEPTH, steps):
        for when, copy in sends(t):
            guarded(when, copy.wait_send)
    first_live = jnp.logical_or(is_even, has_one)
    third_live = jnp.logical_or(even_one, has_two)
    for c in range(CHUNKS):
        for k in range(nw - 1):
            spread(k, c).wait_send()
        guarded(first_live, across(0, c).wait_recv)
        guarded(third_live, across(1, c).wait_recv)


def exchange(white, nb, nw):
    bins, rows, channels = white.shape
    return pl.pallas_call(
        functools.partial(exchange_kernel, nb, nw),
        in_specs=[pl.BlockSpec(memory_space=pl.ANY)],
        out_specs=pl.BlockSpec(memory_space=pl.ANY),
        out_shape=jax.ShapeDtypeStruct(
            (OFFSET + 1, bins // nw, nw * rows, channels), jnp.bfloat16
        ),
        scratch_shapes=[
            pltpu.SemaphoreType.DMA,
            pltpu.SemaphoreType.DMA((nw - 1, CHUNKS)),
            pltpu.SemaphoreType.DMA((nw - 1, CHUNKS)),
            pltpu.SemaphoreType.DMA((2, CHUNKS)),
            pltpu.SemaphoreType.DMA((2, CHUNKS)),
            pltpu.SemaphoreType.DMA((2, CHUNKS)),
            pltpu.SemaphoreType.DMA((2, CHUNKS)),
        ],
        compiler_params=pltpu.CompilerParams(
            collective_id=0, has_side_effects=True, vmem_limit_bytes=SMALL_LIMIT
        ),
        name="exchange",
    )(white)


def cross_kernel(half, windows, offsets_ref, count_ref, own_ref, *refs):
    partners, out_ref = refs[:-1], refs[-1]
    scales = [
        jnp.where(s < count_ref[0], 1.0 / windows, 0.0).astype(jnp.float32)
        for s in range(len(partners))
    ]
    depth, channels = own_ref.shape[2], own_ref.shape[3]
    for b in range(own_ref.shape[1]):
        left = own_ref[0, b].astype(jnp.float32).T.astype(jnp.bfloat16)
        for s, partner in enumerate(partners):
            right = partner[0, b].astype(jnp.float32) * scales[s]
            split = right.reshape(depth // (2 * half), 2, half, channels)
            turned = jnp.stack([-split[:, 1], split[:, 0]], axis=1).reshape(depth, channels)
            right = jnp.concatenate([right, turned], axis=1).astype(jnp.bfloat16)
            value = jnp.dot(left, right, preferred_element_type=jnp.float32)
            value = value.astype(jnp.bfloat16)
            out_ref[s, b, 0] = value[:, :channels]
            out_ref[s, b, 1] = value[:, channels:]


def cross(near, pair_offsets, pair_count, wins):
    _, bins_dev, depth, channels = near.shape
    slots = pair_offsets.shape[0]

    def partner_spec(s):
        return pl.BlockSpec(
            (1, BIN_BLOCK, depth, channels), lambda i, offsets, count: (offsets[s], i, 0, 0)
        )

    return pl.pallas_call(
        functools.partial(cross_kernel, wins, depth // 2),
        grid_spec=pltpu.PrefetchScalarGridSpec(
            num_scalar_prefetch=2,
            grid=(bins_dev // BIN_BLOCK,),
            in_specs=[
                pl.BlockSpec((1, BIN_BLOCK, depth, channels), lambda i, offsets, count: (0, i, 0, 0))
            ]
            + [partner_spec(s) for s in range(slots)],
            out_specs=pl.BlockSpec(
                (slots, BIN_BLOCK, 2, channels, channels),
                lambda i, offsets, count: (0, i, 0, 0, 0),
            ),
        ),
        out_shape=jax.ShapeDtypeStruct((slots, bins_dev, 2, channels, channels), jnp.bfloat16),
        compiler_params=pltpu.CompilerParams(vmem_limit_bytes=CROSS_LIMIT),
        name="cross",
    )(pair_offsets, pair_count, *([near] * (slots + 1)))


def shards(nb, nw, samples, pair_offsets, pair_count):
    white = whiten(samples)
    near = exchange(white, nb, nw)
    return cross(near, pair_offsets, pair_count, samples.shape[1])


def solution(mesh):
    body = functools.partial(shards, mesh.shape["blk"], mesh.shape["win"])
    in_specs = (P("blk", "win", None), P("blk"), P("blk"))
    out_specs = P("blk", "win", None, None, None)
    return jax.shard_map(body, mesh=mesh, in_specs=in_specs, out_specs=out_specs, check_vma=False)
```

```python
import functools
import math

import jax
import jax.numpy as jnp
import ml_dtypes
import numpy as np
from jax import lax
from jax.experimental import pallas as pl
from jax.experimental.pallas import tpu as pltpu
from jax.sharding import PartitionSpec as P

BINS = 128
BIN0 = 32
SMOOTH = 4
OFFSET = 4

WATER_LEVEL = 0.1
EPSILON = 1e-06

ROW_STEPS = 2
CHUNKS = 8
AHEAD = 2
LAG = 3
DEPTH = 2
BIN_BLOCK = 16
CROSS_LIMIT = 40 * 1024 * 1024
SMALL_LIMIT = 24 * 1024 * 1024
MESH = pl.DeviceIdType.MESH


def dft_table(length):
    sample_idx = np.arange(length, dtype=np.int64)
    bin_freqs = BIN0 + np.arange(BINS, dtype=np.int64)
    angles = (sample_idx[:, None] * bin_freqs[None, :] % length) * (2.0 * math.pi / length)
    taper = 0.5 - 0.5 * np.cos((sample_idx + 0.5) * (2.0 * math.pi / length))
    table = np.concatenate(
        [taper[:, None] * np.cos(angles), -taper[:, None] * np.sin(angles)], axis=1
    )
    return table.astype(np.float32).astype(ml_dtypes.bfloat16)


def band_weights():
    source = lax.broadcasted_iota(jnp.int32, (BINS, 2 * BINS), 0)
    target = lax.broadcasted_iota(jnp.int32, (BINS, 2 * BINS), 1)
    inside = jnp.logical_or(jnp.abs(source - target) <= SMOOTH, target >= BINS)
    return jnp.where(inside, 1.0, 0.0).astype(jnp.bfloat16)


def band_scale():
    bin_index = lax.broadcasted_iota(jnp.int32, (1, 2 * BINS), 1)
    inside = jnp.minimum(bin_index, SMOOTH) + jnp.minimum(BINS - 1 - bin_index, SMOOTH) + 1
    share = 1.0 / jnp.maximum(inside, 1).astype(jnp.float32)
    return jnp.where(bin_index < BINS, share, WATER_LEVEL / BINS)


def whiten(wins, copies, samples, table, white, turned, out):
    channels = white.shape[1] // wins
    rows = samples.shape[0] // ROW_STEPS
    weights, scale = band_weights(), band_scale()
    for step in range(ROW_STEPS):
        copies[step].wait()
        here = pl.ds(step * rows, rows)
        spectrum = jnp.dot(samples[here, :], table[...], preferred_element_type=jnp.float32)
        real, imag = spectrum[:, :BINS], spectrum[:, BINS:]
        energy = real * real + imag * imag
        high = energy.astype(jnp.bfloat16)
        low = (energy - high.astype(jnp.float32)).astype(jnp.bfloat16)
        sums = jnp.dot(high, weights, preferred_element_type=jnp.float32)
        sums += jnp.dot(low, weights, preferred_element_type=jnp.float32)
        sums *= scale
        factor = lax.rsqrt(sums[:, :BINS] + sums[:, BINS:] + EPSILON)
        white[0, here, :] = real * factor
        white[1, here, :] = imag * factor
    for part in range(2):
        for win in range(wins):
            piece = white[part, pl.ds(win, channels, stride=wins), :]
            turned[pl.ds(part * wins + win, BINS, stride=2 * wins), :] = piece.T
    out[...] = turned[...].reshape(out.shape).astype(jnp.bfloat16)


def exchange_kernel(
    nb, nw, wins, samples_ref, table_ref, near_ref, samples, table, white, turned, send_ref,
    load_sem, table_sem, home_sem, a_send, a_recv, z_send, z_recv, x_send, x_recv
):
    load_rows = samples.shape[0] // ROW_STEPS
    table_load = pltpu.make_async_copy(table_ref, table, table_sem)
    table_load.start()
    loads = []
    for step in range(ROW_STEPS):
        here = pl.ds(step * load_rows, load_rows)
        loads.append(
            pltpu.make_async_copy(samples_ref.at[here], samples.at[here], load_sem.at[step])
        )
        loads[step].start()
    worker, group = lax.axis_index("blk"), lax.axis_index("win")
    level, odd = lax.div(worker, 2), lax.rem(worker, 2)
    levels = nb // 2
    partner = worker + 1 - 2 * odd
    has_below = level >= 1
    has_one = level + 1 < levels
    has_two = level + 2 < levels
    is_even, is_odd = odd == 0, odd == 1
    bins_dev = near_ref.shape[1]
    rows = send_ref.shape[1]
    size = bins_dev // CHUNKS

    barrier = pltpu.get_barrier_semaphore()

    def greet(device):
        pl.semaphore_signal(barrier, inc=1, device_id=device, device_id_type=MESH)

    peers = [lax.rem(group + k, nw) for k in range(1, nw)]
    for peer in peers:
        greet({"win": peer})
    greet({"blk": partner})

    @pl.when(has_below)
    def _():
        greet({"blk": worker - 2})

    @pl.when(has_one)
    def _():
        greet({"blk": worker + 2})

    table_load.wait()
    whiten(wins, loads, samples, table, white, turned, send_ref)

    my_rows = pl.ds(pl.multiple_of(group * rows, rows), rows)
    home = pltpu.make_async_copy(
        send_ref.at[pl.ds(group * bins_dev, bins_dev)], near_ref.at[0, :, my_rows], home_sem
    )
    home.start()
    pl.semaphore_wait(barrier, nw + has_below.astype(jnp.int32) + has_one.astype(jnp.int32))

    def spread(k, c):
        return pltpu.make_async_remote_copy(
            src_ref=send_ref.at[pl.ds(peers[k] * bins_dev + c * size, size)],
            dst_ref=near_ref.at[0, pl.ds(c * size, size), my_rows],
            send_sem=a_send.at[k, c],
            recv_sem=a_recv.at[k, c],
            device_id={"win": peers[k]},
            device_id_type=MESH,
        )

    def move(src, dst, device, send, recv, at, c):
        return pltpu.make_async_remote_copy(
            src_ref=near_ref.at[src, pl.ds(c * size, size)],
            dst_ref=near_ref.at[dst, pl.ds(c * size, size)],
            send_sem=send.at[at, c],
            recv_sem=recv.at[at, c],
            device_id={"blk": device},
            device_id_type=MESH,
        )

    def down(at, c):
        return move(2 * at, 2 * at + 2, worker - 2, z_send, z_recv, at, c)

    def across(at, c):
        return move(2 * at + 2 * (1 - odd), 2 * at + 1, partner, x_send, x_recv, at, c)

    both = jnp.logical_and(has_below, has_one)
    odd_one = jnp.logical_and(is_odd, has_one)
    even_one = jnp.logical_and(is_even, has_one)
    even_two = jnp.logical_and(is_even, has_two)
    items = 2 * CHUNKS

    def sends(t):
        found = []
        if 0 <= t < items:
            at, c = divmod(t, CHUNKS)
            found.append(((has_below, both)[at], down(at, c)))
            found.append(((is_odd, odd_one)[at], across(at, c)))
        if 0 <= t - LAG < items:
            at, c = divmod(t - LAG, CHUNKS)
            found.append(((even_one, even_two)[at], across(at, c)))
        return found

    def guarded(when, action):
        @pl.when(when)
        def _():
            action()

    def start_spread(c):
        if c < CHUNKS:
            for k in range(nw - 1):
                spread(k, c).start()

    for c in range(AHEAD):
        start_spread(c)
    home.wait()
    steps = items + LAG
    for t in range(steps):
        if t < CHUNKS:
            start_spread(t + AHEAD)
            for k in range(nw - 1):
                spread(k, t).wait_recv()
        if 0 <= t - LAG < items:
            at, c = divmod(t - LAG, CHUNKS)
            guarded((has_one, has_two)[at], down(at, c).wait_recv)
        for when, copy in sends(t - DEPTH):
            guarded(when, copy.wait_send)
        for when, copy in sends(t):
            guarded(when, copy.start)
    for t in range(steps - DEPTH, steps):
        for when, copy in sends(t):
            guarded(when, copy.wait_send)
    first_live = jnp.logical_or(is_even, has_one)
    third_live = jnp.logical_or(even_one, has_two)
    for c in range(CHUNKS):
        for k in range(nw - 1):
            spread(k, c).wait_send()
        guarded(first_live, across(0, c).wait_recv)
        guarded(third_live, across(1, c).wait_recv)


def exchange(samples, nb, nw):
    channels, wins, length = samples.shape
    all_rows, rows = channels * wins, 2 * wins
    return pl.pallas_call(
        functools.partial(exchange_kernel, nb, nw, wins),
        in_specs=[pl.BlockSpec(memory_space=pltpu.HBM)] * 2,
        out_specs=pl.BlockSpec(memory_space=pltpu.VMEM),
        out_shape=jax.ShapeDtypeStruct(
            (OFFSET + 1, BINS // nw, nw * rows, channels), jnp.bfloat16
        ),
        scratch_shapes=[
            pltpu.VMEM((all_rows, length), jnp.bfloat16),
            pltpu.VMEM((length, 2 * BINS), jnp.bfloat16),
            pltpu.VMEM((2, all_rows, BINS), jnp.float32),
            pltpu.VMEM((BINS * rows, channels), jnp.float32),
            pltpu.VMEM((BINS, rows, channels), jnp.bfloat16),
            pltpu.SemaphoreType.DMA((ROW_STEPS,)),
            pltpu.SemaphoreType.DMA,
            pltpu.SemaphoreType.DMA,
            pltpu.SemaphoreType.DMA((nw - 1, CHUNKS)),
            pltpu.SemaphoreType.DMA((nw - 1, CHUNKS)),
            pltpu.SemaphoreType.DMA((2, CHUNKS)),
            pltpu.SemaphoreType.DMA((2, CHUNKS)),
            pltpu.SemaphoreType.DMA((2, CHUNKS)),
            pltpu.SemaphoreType.DMA((2, CHUNKS)),
        ],
        compiler_params=pltpu.CompilerParams(
            collective_id=0, has_side_effects=True, vmem_limit_bytes=SMALL_LIMIT
        ),
        name="exchange",
    )(samples.reshape(all_rows, length), jnp.asarray(dft_table(length)))


def cross_kernel(half, windows, offsets_ref, count_ref, own_ref, *refs):
    partners, out_ref = refs[:-1], refs[-1]
    scales = [
        jnp.where(s < count_ref[0], 1.0 / windows, 0.0).astype(jnp.float32)
        for s in range(len(partners))
    ]
    depth, channels = own_ref.shape[2], own_ref.shape[3]
    for b in range(own_ref.shape[1]):
        left = own_ref[0, b].astype(jnp.float32).T.astype(jnp.bfloat16)
        for s, partner in enumerate(partners):
            right = partner[0, b].astype(jnp.float32) * scales[s]
            split = right.reshape(depth // (2 * half), 2, half, channels)
            turned = jnp.stack([-split[:, 1], split[:, 0]], axis=1).reshape(depth, channels)
            right = jnp.concatenate([right, turned], axis=1).astype(jnp.bfloat16)
            value = jnp.dot(left, right, preferred_element_type=jnp.float32)
            value = value.astype(jnp.bfloat16)
            out_ref[s, b, 0] = value[:, :channels]
            out_ref[s, b, 1] = value[:, channels:]


def cross(near, pair_offsets, pair_count, wins):
    _, bins_dev, depth, channels = near.shape
    slots = pair_offsets.shape[0]

    def partner_spec(s):
        return pl.BlockSpec(
            (1, BIN_BLOCK, depth, channels), lambda i, offsets, count: (offsets[s], i, 0, 0)
        )

    return pl.pallas_call(
        functools.partial(cross_kernel, wins, depth // 2),
        grid_spec=pltpu.PrefetchScalarGridSpec(
            num_scalar_prefetch=2,
            grid=(bins_dev // BIN_BLOCK,),
            in_specs=[
                pl.BlockSpec((1, BIN_BLOCK, depth, channels), lambda i, offsets, count: (0, i, 0, 0))
            ]
            + [partner_spec(s) for s in range(slots)],
            out_specs=pl.BlockSpec(
                (slots, BIN_BLOCK, 2, channels, channels),
                lambda i, offsets, count: (0, i, 0, 0, 0),
            ),
        ),
        out_shape=jax.ShapeDtypeStruct((slots, bins_dev, 2, channels, channels), jnp.bfloat16),
        compiler_params=pltpu.CompilerParams(vmem_limit_bytes=CROSS_LIMIT),
        name="cross",
    )(pair_offsets, pair_count, *([near] * (slots + 1)))


def shards(nb, nw, samples, pair_offsets, pair_count):
    near = exchange(samples, nb, nw)
    return cross(near, pair_offsets, pair_count, samples.shape[1])


def solution(mesh):
    body = functools.partial(shards, mesh.shape["blk"], mesh.shape["win"])
    in_specs = (P("blk", "win", None), P("blk"), P("blk"))
    out_specs = P("blk", "win", None, None, None)
    return jax.shard_map(body, mesh=mesh, in_specs=in_specs, out_specs=out_specs, check_vma=False)
```

```python
import functools
import math

import jax
import jax.numpy as jnp
import ml_dtypes
import numpy as np
from jax import lax
from jax.experimental import pallas as pl
from jax.experimental.pallas import tpu as pltpu
from jax.sharding import PartitionSpec as P

BINS = 128
BIN0 = 32
SMOOTH = 4
OFFSET = 4

WATER_LEVEL = 0.1
EPSILON = 1e-06

ROW_STEPS = 1
CHUNKS = 8
AHEAD = 2
LAG = 4
DEPTH = 2
BIN_BLOCK = 16
CROSS_LIMIT = 40 * 1024 * 1024
SMALL_LIMIT = 24 * 1024 * 1024
MESH = pl.DeviceIdType.MESH


def dft_table(length):
    sample_idx = np.arange(length, dtype=np.int64)
    bin_freqs = BIN0 + np.arange(BINS, dtype=np.int64)
    angles = (sample_idx[:, None] * bin_freqs[None, :] % length) * (2.0 * math.pi / length)
    taper = 0.5 - 0.5 * np.cos((sample_idx + 0.5) * (2.0 * math.pi / length))
    table = np.concatenate(
        [taper[:, None] * np.cos(angles), -taper[:, None] * np.sin(angles)], axis=1
    )
    return table.astype(np.float32).astype(ml_dtypes.bfloat16)


def band_weights():
    source = lax.broadcasted_iota(jnp.int32, (BINS, 2 * BINS), 0)
    target = lax.broadcasted_iota(jnp.int32, (BINS, 2 * BINS), 1)
    inside = jnp.logical_or(jnp.abs(source - target) <= SMOOTH, target >= BINS)
    return jnp.where(inside, 1.0, 0.0).astype(jnp.bfloat16)


def band_scale():
    bin_index = lax.broadcasted_iota(jnp.int32, (1, 2 * BINS), 1)
    inside = jnp.minimum(bin_index, SMOOTH) + jnp.minimum(BINS - 1 - bin_index, SMOOTH) + 1
    share = 1.0 / jnp.maximum(inside, 1).astype(jnp.float32)
    return jnp.where(bin_index < BINS, share, WATER_LEVEL / BINS)


def whiten(wins, copies, samples, table, white, turned, out):
    channels = white.shape[1] // wins
    rows = samples.shape[0] // ROW_STEPS
    weights, scale = band_weights(), band_scale()
    for step in range(ROW_STEPS):
        copies[step].wait()
        here = pl.ds(step * rows, rows)
        spectrum = jnp.dot(samples[here, :], table[...], preferred_element_type=jnp.float32)
        real, imag = spectrum[:, :BINS], spectrum[:, BINS:]
        energy = real * real + imag * imag
        high = energy.astype(jnp.bfloat16)
        low = (energy - high.astype(jnp.float32)).astype(jnp.bfloat16)
        sums = jnp.dot(high, weights, preferred_element_type=jnp.float32)
        sums += jnp.dot(low, weights, preferred_element_type=jnp.float32)
        sums *= scale
        factor = lax.rsqrt(sums[:, :BINS] + sums[:, BINS:] + EPSILON)
        white[0, here, :] = real * factor
        white[1, here, :] = imag * factor
    for part in range(2):
        for win in range(wins):
            piece = white[part, pl.ds(win, channels, stride=wins), :]
            turned[pl.ds(part * wins + win, BINS, stride=2 * wins), :] = piece.T
    out[...] = turned[...].reshape(out.shape).astype(jnp.bfloat16)


def exchange_kernel(
    nb, nw, wins, samples_ref, table_ref, near_ref, samples, table, white, turned, send_ref,
    load_sem, table_sem, home_sem, a_send, a_recv, z_send, z_recv, x_send, x_recv
):
    load_rows = samples.shape[0] // ROW_STEPS
    table_load = pltpu.make_async_copy(table_ref, table, table_sem)
    table_load.start()
    loads = []
    for step in range(ROW_STEPS):
        here = pl.ds(step * load_rows, load_rows)
        loads.append(
            pltpu.make_async_copy(samples_ref.at[here], samples.at[here], load_sem.at[step])
        )
        loads[step].start()
    worker, group = lax.axis_index("blk"), lax.axis_index("win")
    level, odd = lax.div(worker, 2), lax.rem(worker, 2)
    levels = nb // 2
    partner = worker + 1 - 2 * odd
    has_below = level >= 1
    has_one = level + 1 < levels
    has_two = level + 2 < levels
    is_even, is_odd = odd == 0, odd == 1
    bins_dev = near_ref.shape[1]
    rows = send_ref.shape[1]
    size = bins_dev // CHUNKS

    barrier = pltpu.get_barrier_semaphore()

    def greet(device):
        pl.semaphore_signal(barrier, inc=1, device_id=device, device_id_type=MESH)

    peers = [lax.rem(group + k, nw) for k in range(1, nw)]
    for peer in peers:
        greet({"win": peer})
    greet({"blk": partner})

    @pl.when(has_below)
    def _():
        greet({"blk": worker - 2})

    @pl.when(has_one)
    def _():
        greet({"blk": worker + 2})

    table_load.wait()
    whiten(wins, loads, samples, table, white, turned, send_ref)

    my_rows = pl.ds(pl.multiple_of(group * rows, rows), rows)
    home = pltpu.make_async_copy(
        send_ref.at[pl.ds(group * bins_dev, bins_dev)], near_ref.at[0, :, my_rows], home_sem
    )
    home.start()
    pl.semaphore_wait(barrier, nw + has_below.astype(jnp.int32) + has_one.astype(jnp.int32))

    def spread(k, c):
        return pltpu.make_async_remote_copy(
            src_ref=send_ref.at[pl.ds(peers[k] * bins_dev + c * size, size)],
            dst_ref=near_ref.at[0, pl.ds(c * size, size), my_rows],
            send_sem=a_send.at[k, c],
            recv_sem=a_recv.at[k, c],
            device_id={"win": peers[k]},
            device_id_type=MESH,
        )

    def move(src, dst, device, send, recv, at, c):
        return pltpu.make_async_remote_copy(
            src_ref=near_ref.at[src, pl.ds(c * size, size)],
            dst_ref=near_ref.at[dst, pl.ds(c * size, size)],
            send_sem=send.at[at, c],
            recv_sem=recv.at[at, c],
            device_id={"blk": device},
            device_id_type=MESH,
        )

    def down(at, c):
        return move(2 * at, 2 * at + 2, worker - 2, z_send, z_recv, at, c)

    def across(at, c):
        return move(2 * at + 2 * (1 - odd), 2 * at + 1, partner, x_send, x_recv, at, c)

    both = jnp.logical_and(has_below, has_one)
    odd_one = jnp.logical_and(is_odd, has_one)
    even_one = jnp.logical_and(is_even, has_one)
    even_two = jnp.logical_and(is_even, has_two)
    items = 2 * CHUNKS

    def sends(t):
        found = []
        if 0 <= t < items:
            at, c = divmod(t, CHUNKS)
            found.append(((has_below, both)[at], down(at, c)))
            found.append(((is_odd, odd_one)[at], across(at, c)))
        if 0 <= t - LAG < items:
            at, c = divmod(t - LAG, CHUNKS)
            found.append(((even_one, even_two)[at], across(at, c)))
        return found

    def guarded(when, action):
        @pl.when(when)
        def _():
            action()

    def start_spread(c):
        if c < CHUNKS:
            for k in range(nw - 1):
                spread(k, c).start()

    for c in range(AHEAD):
        start_spread(c)
    home.wait()
    steps = items + LAG
    for t in range(steps):
        if t < CHUNKS:
            start_spread(t + AHEAD)
            for k in range(nw - 1):
                spread(k, t).wait_recv()
        if 0 <= t - LAG < items:
            at, c = divmod(t - LAG, CHUNKS)
            guarded((has_one, has_two)[at], down(at, c).wait_recv)
        for when, copy in sends(t - DEPTH):
            guarded(when, copy.wait_send)
        for when, copy in sends(t):
            guarded(when, copy.start)
    for t in range(steps - DEPTH, steps):
        for when, copy in sends(t):
            guarded(when, copy.wait_send)
    first_live = jnp.logical_or(is_even, has_one)
    third_live = jnp.logical_or(even_one, has_two)
    for c in range(CHUNKS):
        for k in range(nw - 1):
            spread(k, c).wait_send()
        guarded(first_live, across(0, c).wait_recv)
        guarded(third_live, across(1, c).wait_recv)


def exchange(samples, nb, nw):
    channels, wins, length = samples.shape
    all_rows, rows = channels * wins, 2 * wins
    return pl.pallas_call(
        functools.partial(exchange_kernel, nb, nw, wins),
        in_specs=[pl.BlockSpec(memory_space=pltpu.HBM)] * 2,
        out_specs=pl.BlockSpec(memory_space=pltpu.VMEM),
        out_shape=jax.ShapeDtypeStruct(
            (OFFSET + 1, BINS // nw, nw * rows, channels), jnp.bfloat16
        ),
        scratch_shapes=[
            pltpu.VMEM((all_rows, length), jnp.bfloat16),
            pltpu.VMEM((length, 2 * BINS), jnp.bfloat16),
            pltpu.VMEM((2, all_rows, BINS), jnp.float32),
            pltpu.VMEM((BINS * rows, channels), jnp.float32),
            pltpu.VMEM((BINS, rows, channels), jnp.bfloat16),
            pltpu.SemaphoreType.DMA((ROW_STEPS,)),
            pltpu.SemaphoreType.DMA,
            pltpu.SemaphoreType.DMA,
            pltpu.SemaphoreType.DMA((nw - 1, CHUNKS)),
            pltpu.SemaphoreType.DMA((nw - 1, CHUNKS)),
            pltpu.SemaphoreType.DMA((2, CHUNKS)),
            pltpu.SemaphoreType.DMA((2, CHUNKS)),
            pltpu.SemaphoreType.DMA((2, CHUNKS)),
            pltpu.SemaphoreType.DMA((2, CHUNKS)),
        ],
        compiler_params=pltpu.CompilerParams(
            collective_id=0, has_side_effects=True, vmem_limit_bytes=SMALL_LIMIT
        ),
        name="exchange",
    )(samples.reshape(all_rows, length), jnp.asarray(dft_table(length)))


def cross_kernel(half, windows, offsets_ref, count_ref, own_ref, *refs):
    partners, out_ref = refs[:-1], refs[-1]
    scales = [
        jnp.where(s < count_ref[0], 1.0 / windows, 0.0).astype(jnp.float32)
        for s in range(len(partners))
    ]
    depth, channels = own_ref.shape[2], own_ref.shape[3]
    for b in range(own_ref.shape[1]):
        left = own_ref[0, b].astype(jnp.float32).T.astype(jnp.bfloat16)
        for s, partner in enumerate(partners):
            right = partner[0, b].astype(jnp.float32) * scales[s]
            split = right.reshape(depth // (2 * half), 2, half, channels)
            turned = jnp.stack([-split[:, 1], split[:, 0]], axis=1).reshape(depth, channels)
            right = jnp.concatenate([right, turned], axis=1).astype(jnp.bfloat16)
            value = jnp.dot(left, right, preferred_element_type=jnp.float32)
            value = value.astype(jnp.bfloat16)
            out_ref[s, b, 0] = value[:, :channels]
            out_ref[s, b, 1] = value[:, channels:]


def cross(near, pair_offsets, pair_count, wins):
    _, bins_dev, depth, channels = near.shape
    slots = pair_offsets.shape[0]

    def partner_spec(s):
        return pl.BlockSpec(
            (1, BIN_BLOCK, depth, channels), lambda i, offsets, count: (offsets[s], i, 0, 0)
        )

    return pl.pallas_call(
        functools.partial(cross_kernel, wins, depth // 2),
        grid_spec=pltpu.PrefetchScalarGridSpec(
            num_scalar_prefetch=2,
            grid=(bins_dev // BIN_BLOCK,),
            in_specs=[
                pl.BlockSpec((1, BIN_BLOCK, depth, channels), lambda i, offsets, count: (0, i, 0, 0))
            ]
            + [partner_spec(s) for s in range(slots)],
            out_specs=pl.BlockSpec(
                (slots, BIN_BLOCK, 2, channels, channels),
                lambda i, offsets, count: (0, i, 0, 0, 0),
            ),
        ),
        out_shape=jax.ShapeDtypeStruct((slots, bins_dev, 2, channels, channels), jnp.bfloat16),
        compiler_params=pltpu.CompilerParams(vmem_limit_bytes=CROSS_LIMIT),
        name="cross",
    )(pair_offsets, pair_count, *([near] * (slots + 1)))


def shards(nb, nw, samples, pair_offsets, pair_count):
    near = exchange(samples, nb, nw)
    return cross(near, pair_offsets, pair_count, samples.shape[1])


def solution(mesh):
    body = functools.partial(shards, mesh.shape["blk"], mesh.shape["win"])
    in_specs = (P("blk", "win", None), P("blk"), P("blk"))
    out_specs = P("blk", "win", None, None, None)
    return jax.shard_map(body, mesh=mesh, in_specs=in_specs, out_specs=out_specs, check_vma=False)
```
